32 devices in a mesh: space: 8 (over z, x), var: 4 (over y, core).
Axes of the slice: x: 2, y: 2, z: 4, core: 2. Of those that a mesh axis runs over, the one named last changes fastest.
Arguments:
- tensor_field: bfloat16 [128, 262144], P('var', 'space'), may hold values from -32 to 32
- start_basis: float32 [128, 32], replicated, may hold values from -5 to 5
Outputs:
- leading_basis: float32 [128, 32], replicated
- core_tensor: float32 [32, 262144], P(None, ('space', 'var'))
The draws below stay inside these ranges and needn't reach their ends.
All inputs are finite; a program needn't handle non-finite values.
Results may differ from the reference program's by a relative error of at most 0.0024.
Values may be sent and summed in bfloat16 or wider, within the bound.
A program may use at most 64 MiB of HBM per device.

```python
import jax
import jax.numpy as jnp
from jax import lax

V = 128
R = 32
ITERS = 8
CELLS = 262144


def draw_tensor_field(key, part):
    key = jax.random.fold_in(key, 11)
    key_rows, key_cells, key_loads, key_latent, key_noise = jax.random.split(key, 5)
    row_scale = jnp.exp(jax.random.uniform(key_rows, (V, 1), jnp.float32, jnp.log(0.6), jnp.log(1.7)))
    cell_scale = jnp.exp(jax.random.uniform(key_cells, (1, CELLS), jnp.float32, jnp.log(0.5), jnp.log(2.0)))
    loadings = jax.random.uniform(key_loads, (V, 1), jnp.float32, -1.2, 1.2)
    latent = jnp.clip(jax.random.normal(key_latent, (8, CELLS), jnp.float32), -4.0, 4.0)
    latent_index = jnp.arange(V) % 8
    spread = latent[latent_index]
    own_noise = jnp.clip(jax.random.normal(key_noise, (V, CELLS), jnp.float32), -4.0, 4.0)
    drawn = row_scale * cell_scale * (own_noise + loadings * spread)
    return drawn.astype(jnp.bfloat16)


def centred(key, extent, deviation, reach, kind=jnp.bfloat16):
    values = deviation * jax.random.normal(key, extent, jnp.float32)
    return jnp.clip(values, min=-reach, max=reach).astype(kind)


def setup_inputs(seed: int = 0) -> dict:
    arg_keys = jax.random.split(jax.random.key(seed), 3)
    return {
        "tensor_field": draw_tensor_field(jax.random.fold_in(arg_keys[2], 71), 0),
        "start_basis": centred(arg_keys[1], (V, R), 1.0, 5.0, jnp.float32),
    }


def orthonormal(product):
    cross_gram = jnp.dot(product.T.astype(jnp.float32), product.astype(jnp.float32), precision=lax.Precision.HIGHEST, preferred_element_type=jnp.float32)
    factor = jnp.linalg.cholesky(cross_gram)
    return lax.linalg.triangular_solve(factor, product.T, left_side=True, lower=True).T

def reference(tensor_field, start_basis):
    gram_matrix = jnp.dot(tensor_field.astype(jnp.float32), tensor_field.T.astype(jnp.float32), preferred_element_type=jnp.float32)
    leading_basis = start_basis
    for iteration in range(ITERS):
        product = jnp.dot(gram_matrix.astype(jnp.float32), leading_basis.astype(jnp.float32), precision=lax.Precision.HIGHEST, preferred_element_type=jnp.float32)
        leading_basis = orthonormal(product)
    narrow = leading_basis.astype(jnp.bfloat16)
    core_tensor = jnp.dot(narrow.T.astype(jnp.float32), tensor_field.astype(jnp.float32), preferred_element_type=jnp.float32)
    return (leading_basis, core_tensor)
```

```python
import jax
import jax.numpy as jnp
from jax import lax
from jax.experimental import pallas as pl
from jax.experimental.pallas import tpu as pltpu
from jax.sharding import PartitionSpec as P

ITERS = 8
SUB = 8


def eliminate(cross_gram, rows):
    rank, width = rows.shape
    blocks = rank // SUB
    rows = [rows[b * SUB : (b + 1) * SUB] for b in range(blocks)]
    columns = [
        [
            jnp.broadcast_to(cross_gram[b * SUB : (b + 1) * SUB, k : k + 1], (SUB, width))
            if b >= k // SUB
            else None
            for b in range(blocks)
        ]
        for k in range(rank)
    ]
    place = lax.broadcasted_iota(jnp.int32, (SUB, width), 0)
    pivots = [jnp.ones((SUB, width), jnp.float32) for _ in range(blocks)]
    for j in range(rank):
        home, spot = divmod(j, SUB)
        column = columns[j]
        pivot = jnp.broadcast_to(column[home][spot : spot + 1], (SUB, width))
        pivots[home] = jnp.where(place == spot, pivot, pivots[home])
        inverse = 1.0 / pivot
        scaled = [None] * blocks
        for b in range(home, blocks):
            scaled[b] = column[b] * inverse
        scaled[home] = jnp.where(place > spot, scaled[home], 0.0)
        for k in range(j + 1, rank):
            other = jnp.broadcast_to(column[k // SUB][k % SUB : k % SUB + 1], (SUB, width))
            for b in range(k // SUB, blocks):
                columns[k][b] = columns[k][b] - scaled[b] * other
        row = jnp.broadcast_to(rows[home][spot : spot + 1], (SUB, width))
        for b in range(home, blocks):
            rows[b] = rows[b] - scaled[b] * row
    return jnp.concatenate([rows[b] * lax.rsqrt(pivots[b]) for b in range(blocks)], axis=0)


def dot(a, b, transposed=False):
    return lax.dot_general(
        a,
        b,
        (((1,), (1 if transposed else 0,)), ((), ())),
        precision=lax.Precision.HIGHEST,
        preferred_element_type=jnp.float32,
    )


def iterate(gram, basis):
    product = dot(basis.T, gram)

    def step(_, product):
        return eliminate(dot(product, product, True), dot(product, gram))

    product = lax.fori_loop(0, ITERS - 1, step, product)
    return eliminate(dot(product, product, True), product)


def basis_kernel(gram_ref, start_ref, basis_ref, narrow_ref):
    basis = iterate(gram_ref[...], start_ref[...])
    basis_ref[...] = basis.T
    narrow_ref[...] = basis.astype(jnp.bfloat16)


def per_device(tensor_field, start_basis):
    fibres = lax.all_to_all(tensor_field, "var", split_axis=1, concat_axis=0, tiled=True)
    partial_gram = jnp.einsum("vc,wc->vw", fibres, fibres, preferred_element_type=jnp.float32)
    gram_matrix = lax.psum(partial_gram, ("space", "var"))
    variables, rank = start_basis.shape
    leading_basis, narrow = pl.pallas_call(
        basis_kernel,
        out_shape=(
            jax.ShapeDtypeStruct((variables, rank), jnp.float32),
            jax.ShapeDtypeStruct((rank, variables), jnp.bfloat16),
        ),
    )(gram_matrix, start_basis)
    core_tensor = jnp.dot(narrow, fibres, preferred_element_type=jnp.float32)
    return (leading_basis, core_tensor)


def solution(mesh):
    return jax.shard_map(
        per_device,
        mesh=mesh,
        in_specs=(P("var", "space"), P()),
        out_specs=(P(), P(None, ("space", "var"))),
        check_vma=False,
    )
```

```python
import functools

import jax
import jax.numpy as jnp
from jax import lax
from jax.experimental import pallas as pl
from jax.experimental.pallas import tpu as pltpu
from jax.sharding import PartitionSpec as P

ITERS = 8
SUB = 8
CHUNKS = 4
MESH = pl.DeviceIdType.MESH


def eliminate(cross_gram, rows):
    rank, width = rows.shape
    blocks = rank // SUB
    rows = [rows[b * SUB : (b + 1) * SUB] for b in range(blocks)]
    columns = [
        [
            jnp.broadcast_to(cross_gram[b * SUB : (b + 1) * SUB, k : k + 1], (SUB, width))
            if b >= k // SUB
            else None
            for b in range(blocks)
        ]
        for k in range(rank)
    ]
    place = lax.broadcasted_iota(jnp.int32, (SUB, width), 0)
    pivots = [jnp.ones((SUB, width), jnp.float32) for _ in range(blocks)]
    for j in range(rank):
        home, spot = divmod(j, SUB)
        column = columns[j]
        pivot = jnp.broadcast_to(column[home][spot : spot + 1], (SUB, width))
        pivots[home] = jnp.where(place == spot, pivot, pivots[home])
        inverse = 1.0 / pivot
        scaled = [None] * blocks
        for b in range(home, blocks):
            scaled[b] = column[b] * inverse
        scaled[home] = jnp.where(place > spot, scaled[home], 0.0)
        for k in range(j + 1, rank):
            other = jnp.broadcast_to(column[k // SUB][k % SUB : k % SUB + 1], (SUB, width))
            for b in range(k // SUB, blocks):
                columns[k][b] = columns[k][b] - scaled[b] * other
        row = jnp.broadcast_to(rows[home][spot : spot + 1], (SUB, width))
        for b in range(home, blocks):
            rows[b] = rows[b] - scaled[b] * row
    return jnp.concatenate([rows[b] * lax.rsqrt(pivots[b]) for b in range(blocks)], axis=0)


def dot(a, b, transposed=False):
    return lax.dot_general(
        a,
        b,
        (((1,), (1 if transposed else 0,)), ((), ())),
        precision=lax.Precision.HIGHEST,
        preferred_element_type=jnp.float32,
    )


def iterate(gram, basis):
    product = dot(basis.T, gram)

    def step(_, product):
        return eliminate(dot(product, product, True), dot(product, gram))

    product = lax.fori_loop(0, ITERS - 1, step, product)
    return eliminate(dot(product, product, True), product)


def kernel(
    sizes,
    field_ref,
    start_ref,
    basis_ref,
    core_ref,
    fibres,
    core,
    pieces,
    landed,
    slices,
    whole,
    own_sem,
    core_sem,
    field_send,
    field_recv,
    scatter_send,
    scatter_recv,
    sum_send,
    sum_recv,
    gather_send,
    gather_recv,
):
    n_space, n_var = sizes["space"], sizes["var"]
    me_space, me_var = lax.axis_index("space"), lax.axis_index("var")
    slice_rows = field_ref.shape[0]
    variables, cells = fibres.shape
    width = cells // CHUNKS
    height = variables // n_space

    def ahead(axis, distance):
        return lax.rem(lax.axis_index(axis) + distance, sizes[axis])

    def behind(axis, distance):
        return lax.rem(lax.axis_index(axis) + sizes[axis] - distance, sizes[axis])

    def rows_of(device):
        return pl.ds(pl.multiple_of(device * slice_rows, slice_rows), slice_rows)

    def source(device, chunk):
        start = pl.multiple_of(device * cells + chunk * width, width)
        return field_ref.at[:, pl.ds(start, width)]

    barrier = pltpu.get_barrier_semaphore()
    for axis in ("space", "var"):
        for distance in range(1, sizes[axis]):
            pl.semaphore_signal(
                barrier, inc=1, device_id={axis: ahead(axis, distance)}, device_id_type=MESH
            )
    pl.semaphore_wait(barrier, n_space + n_var - 2)

    own, sends = [], []
    for chunk in range(CHUNKS):
        columns = pl.ds(chunk * width, width)
        for distance in [n_var // 2] + [d for d in range(1, n_var) if d != n_var // 2]:
            peer = ahead("var", distance)
            copy = pltpu.make_async_remote_copy(
                src_ref=source(peer, chunk),
                dst_ref=fibres.at[rows_of(me_var), columns],
                send_sem=field_send.at[chunk, distance],
                recv_sem=field_recv.at[chunk, distance],
                device_id={"var": peer},
                device_id_type=MESH,
            )
            copy.start()
            sends.append(copy)
        copy = pltpu.make_async_copy(
            source(me_var, chunk), fibres.at[rows_of(me_var), columns], own_sem.at[chunk]
        )
        copy.start()
        own.append(copy)

    gram = jnp.zeros((variables, variables), jnp.float32)
    for chunk in range(CHUNKS):
        columns = pl.ds(chunk * width, width)
        own[chunk].wait()
        for distance in range(1, n_var):
            sender = behind("var", distance)
            pltpu.make_async_remote_copy(
                src_ref=source(sender, chunk),
                dst_ref=fibres.at[rows_of(sender), columns],
                send_sem=field_send.at[chunk, distance],
                recv_sem=field_recv.at[chunk, distance],
                device_id={"var": sender},
                device_id_type=MESH,
            ).wait_recv()
        block = fibres[:, columns]
        gram = gram + lax.dot_general(
            block, block, (((1,), (1,)), ((), ())), preferred_element_type=jnp.float32
        )

    def exchange(axis, source_of, into, send, recv):
        mine = lax.axis_index(axis)
        for distance in range(1, sizes[axis]):
            peer = ahead(axis, distance)
            copy = pltpu.make_async_remote_copy(
                src_ref=source_of(peer),
                dst_ref=into.at[mine],
                send_sem=send.at[distance],
                recv_sem=recv.at[distance],
                device_id={axis: peer},
                device_id_type=MESH,
            )
            copy.start()
            sends.append(copy)
        for distance in range(1, sizes[axis]):
            sender = behind(axis, distance)
            pltpu.make_async_remote_copy(
                src_ref=source_of(sender),
                dst_ref=into.at[sender],
                send_sem=send.at[distance],
                recv_sem=recv.at[distance],
                device_id={axis: sender},
                device_id_type=MESH,
            ).wait_recv()

    for s in range(n_space):
        pieces[s] = gram[s * height : (s + 1) * height]
    landed[me_space] = pieces[me_space]
    exchange("space", lambda peer: pieces.at[peer], landed, scatter_send, scatter_recv)
    slices[me_var] = jnp.sum(landed[...], axis=0)
    exchange("var", lambda peer: slices.at[me_var], slices, sum_send, sum_recv)
    whole[me_space] = jnp.sum(slices[...], axis=0)
    exchange("space", lambda peer: whole.at[me_space], whole, gather_send, gather_recv)
    gram = whole[...].reshape(variables, variables)

    basis = iterate(gram, start_ref[...])
    narrow = basis.astype(jnp.bfloat16)
    stores = []
    for chunk in range(CHUNKS):
        columns = pl.ds(chunk * width, width)
        core[:, columns] = jnp.dot(
            narrow, fibres[:, columns], preferred_element_type=jnp.float32
        )
        copy = pltpu.make_async_copy(
            core.at[:, columns], core_ref.at[:, columns], core_sem.at[chunk]
        )
        copy.start()
        stores.append(copy)
    basis_ref[...] = basis.T
    for copy in sends:
        copy.wait_send()
    for copy in stores:
        copy.wait()


def per_device(sizes, tensor_field, start_basis):
    variables, rank = start_basis.shape
    n_space, n_var = sizes["space"], sizes["var"]
    cells = tensor_field.shape[1] // n_var
    height = variables // n_space
    dma = pltpu.SemaphoreType.DMA
    return pl.pallas_call(
        functools.partial(kernel, sizes),
        out_shape=(
            jax.ShapeDtypeStruct((variables, rank), jnp.float32),
            jax.ShapeDtypeStruct((rank, cells), jnp.float32),
        ),
        in_specs=[pl.BlockSpec(memory_space=pl.ANY), pl.BlockSpec(memory_space=pltpu.VMEM)],
        out_specs=(pl.BlockSpec(memory_space=pltpu.VMEM), pl.BlockSpec(memory_space=pl.ANY)),
        scratch_shapes=[
            pltpu.VMEM((variables, cells), jnp.bfloat16),
            pltpu.VMEM((rank, cells), jnp.float32),
            pltpu.VMEM((n_space, height, variables), jnp.float32),
            pltpu.VMEM((n_space, height, variables), jnp.float32),
            pltpu.VMEM((n_var, height, variables), jnp.float32),
            pltpu.VMEM((n_space, height, variables), jnp.float32),
            dma((CHUNKS,)),
            dma((CHUNKS,)),
            dma((CHUNKS, n_var)),
            dma((CHUNKS, n_var)),
            dma((n_space,)),
            dma((n_space,)),
            dma((n_var,)),
            dma((n_var,)),
            dma((n_space,)),
            dma((n_space,)),
        ],
        compiler_params=pltpu.CompilerParams(
            collective_id=0, has_side_effects=True, vmem_limit_bytes=48 * 2**20
        ),
    )(tensor_field, start_basis)


def solution(mesh):
    return jax.shard_map(
        functools.partial(per_device, dict(mesh.shape)),
        mesh=mesh,
        in_specs=(P("var", "space"), P()),
        out_specs=(P(), P(None, ("space", "var"))),
        check_vma=False,
    )
```

```python
import functools

import jax
import jax.numpy as jnp
from jax import lax
from jax.experimental import pallas as pl
from jax.experimental.pallas import tpu as pltpu
from jax.sharding import PartitionSpec as P

ITERS = 8
SUB = 8
CHUNKS = 4
MESH = pl.DeviceIdType.MESH


def eliminate(cross_gram, rows):
    rank, width = rows.shape
    blocks = rank // SUB
    rows = [rows[b * SUB : (b + 1) * SUB] for b in range(blocks)]
    columns = [
        [
            jnp.broadcast_to(cross_gram[b * SUB : (b + 1) * SUB, k : k + 1], (SUB, width))
            if b >= k // SUB
            else None
            for b in range(blocks)
        ]
        for k in range(rank)
    ]
    place = lax.broadcasted_iota(jnp.int32, (SUB, width), 0)
    pivots = [jnp.ones((SUB, width), jnp.float32) for _ in range(blocks)]
    for j in range(rank):
        home, spot = divmod(j, SUB)
        column = columns[j]
        pivot = jnp.broadcast_to(column[home][spot : spot + 1], (SUB, width))
        pivots[home] = jnp.where(place == spot, pivot, pivots[home])
        inverse = 1.0 / pivot
        scaled = [None] * blocks
        for b in range(home, blocks):
            scaled[b] = column[b] * inverse
        scaled[home] = jnp.where(place > spot, scaled[home], 0.0)
        for k in range(j + 1, rank):
            other = jnp.broadcast_to(column[k // SUB][k % SUB : k % SUB + 1], (SUB, width))
            for b in range(k // SUB, blocks):
                columns[k][b] = columns[k][b] - scaled[b] * other
        row = jnp.broadcast_to(rows[home][spot : spot + 1], (SUB, width))
        for b in range(home, blocks):
            rows[b] = rows[b] - scaled[b] * row
    return jnp.concatenate([rows[b] * lax.rsqrt(pivots[b]) for b in range(blocks)], axis=0)


def split(value):
    high = value.astype(jnp.bfloat16)
    rest = value - high.astype(jnp.float32)
    middle = rest.astype(jnp.bfloat16)
    return high, middle, (rest - middle.astype(jnp.float32)).astype(jnp.bfloat16)


def join(terms, order, axis):
    return jnp.concatenate([terms[i] for i in order], axis=axis)


LEFT, RIGHT = (1, 0, 2, 0, 1, 0), (1, 2, 0, 1, 0, 0)


def dot(a, b, axis):
    return lax.dot_general(
        a, b, (((1,), (axis,)), ((), ())), preferred_element_type=jnp.float32
    )


def iterate(gram, basis, split_gram):
    split_gram[...] = join(split(gram), RIGHT, 0)
    product = dot(join(split(basis), LEFT, 1), split_gram[...], 0)

    def step(_, product):
        terms = split(product)
        left = join(terms, LEFT, 1)
        cross_gram = dot(left, join(terms, RIGHT, 1), 1)
        return eliminate(cross_gram, dot(left, split_gram[...], 0))

    product = lax.fori_loop(0, ITERS - 1, step, product)
    terms = split(product)
    return eliminate(dot(join(terms, LEFT, 1), join(terms, RIGHT, 1), 1), product)


def gram_kernel(
    sizes,
    field_ref,
    gram_ref,
    fibres_ref,
    fibres,
    pieces,
    landed,
    slices,
    whole,
    keep_sem,
    own_sem,
    field_send,
    field_recv,
    scatter_send,
    scatter_recv,
    sum_send,
    sum_recv,
    gather_send,
    gather_recv,
):
    n_space, n_var = sizes["space"], sizes["var"]
    me_space, me_var = lax.axis_index("space"), lax.axis_index("var")
    slice_rows = field_ref.shape[0]
    variables, cells = fibres.shape
    width = cells // CHUNKS
    height = variables // n_var

    def ahead(axis, distance):
        return lax.rem(lax.axis_index(axis) + distance, sizes[axis])

    def behind(axis, distance):
        return lax.rem(lax.axis_index(axis) + sizes[axis] - distance, sizes[axis])

    def rows_of(device):
        return pl.ds(pl.multiple_of(device * slice_rows, slice_rows), slice_rows)

    def source(device, chunk):
        start = pl.multiple_of(device * cells + chunk * width, width)
        return field_ref.at[:, pl.ds(start, width)]

    barrier = pltpu.get_barrier_semaphore()
    for axis in ("space", "var"):
        for distance in range(1, sizes[axis]):
            pl.semaphore_signal(
                barrier, inc=1, device_id={axis: ahead(axis, distance)}, device_id_type=MESH
            )
    pl.semaphore_wait(barrier, n_space + n_var - 2)

    own, sends = [], []
    for chunk in range(CHUNKS):
        columns = pl.ds(chunk * width, width)
        for distance in [n_var // 2] + [d for d in range(1, n_var) if d != n_var // 2]:
            peer = ahead("var", distance)
            copy = pltpu.make_async_remote_copy(
                src_ref=source(peer, chunk),
                dst_ref=fibres.at[rows_of(me_var), columns],
                send_sem=field_send.at[chunk, distance],
                recv_sem=field_recv.at[chunk, distance],
                device_id={"var": peer},
                device_id_type=MESH,
            )
            copy.start()
            sends.append(copy)
        copy = pltpu.make_async_copy(
            source(me_var, chunk), fibres.at[rows_of(me_var), columns], own_sem.at[chunk]
        )
        copy.start()
        own.append(copy)

    gram = jnp.zeros((variables, variables), jnp.float32)
    for chunk in range(CHUNKS):
        columns = pl.ds(chunk * width, width)
        own[chunk].wait()
        for distance in range(1, n_var):
            sender = behind("var", distance)
            pltpu.make_async_remote_copy(
                src_ref=source(sender, chunk),
                dst_ref=fibres.at[rows_of(sender), columns],
                send_sem=field_send.at[chunk, distance],
                recv_sem=field_recv.at[chunk, distance],
                device_id={"var": sender},
                device_id_type=MESH,
            ).wait_recv()
        block = fibres[:, columns]
        gram = gram + lax.dot_general(
            block, block, (((1,), (1,)), ((), ())), preferred_element_type=jnp.float32
        )

    keep = pltpu.make_async_copy(fibres, fibres_ref, keep_sem)
    keep.start()

    def exchange(axis, source_of, into, send, recv):
        mine = lax.axis_index(axis)
        for distance in range(1, sizes[axis]):
            peer = ahead(axis, distance)
            copy = pltpu.make_async_remote_copy(
                src_ref=source_of(peer),
                dst_ref=into.at[mine],
                send_sem=send.at[distance],
                recv_sem=recv.at[distance],
                device_id={axis: peer},
                device_id_type=MESH,
            )
            copy.start()
            sends.append(copy)
        for distance in range(1, sizes[axis]):
            sender = behind(axis, distance)
            pltpu.make_async_remote_copy(
                src_ref=source_of(sender),
                dst_ref=into.at[sender],
                send_sem=send.at[distance],
                recv_sem=recv.at[distance],
                device_id={axis: sender},
                device_id_type=MESH,
            ).wait_recv()

    for v in range(n_var):
        pieces[v] = gram[v * height : (v + 1) * height]
    landed[me_var] = pieces[me_var]
    exchange("var", lambda peer: pieces.at[peer], landed, scatter_send, scatter_recv)
    slices[me_space] = jnp.sum(landed[...], axis=0)
    exchange("space", lambda peer: slices.at[me_space], slices, sum_send, sum_recv)
    whole[me_var] = jnp.sum(slices[...], axis=0)
    exchange("var", lambda peer: whole.at[me_var], whole, gather_send, gather_recv)
    gram_ref[...] = whole[...].reshape(variables, variables)
    for copy in sends:
        copy.wait_send()
    keep.wait()


def core_kernel(
    gram_ref, start_ref, fibres_ref, basis_ref, core_ref, fibres, core, split_gram, load_sem, core_sem
):
    load = pltpu.make_async_copy(fibres_ref, fibres, load_sem)
    load.start()
    basis = iterate(gram_ref[...], start_ref[...], split_gram)
    basis_ref[...] = basis
    narrow = basis.astype(jnp.bfloat16)
    load.wait()
    width = fibres.shape[1] // CHUNKS
    stores = []
    for chunk in range(CHUNKS):
        columns = pl.ds(chunk * width, width)
        core[:, columns] = jnp.dot(
            narrow, fibres[:, columns], preferred_element_type=jnp.float32
        )
        copy = pltpu.make_async_copy(
            core.at[:, columns], core_ref.at[:, columns], core_sem.at[chunk]
        )
        copy.start()
        stores.append(copy)
    for copy in stores:
        copy.wait()


def per_device(sizes, tensor_field, start_basis):
    variables, rank = start_basis.shape
    n_space, n_var = sizes["space"], sizes["var"]
    cells = tensor_field.shape[1] // n_var
    height = variables // n_var
    dma = pltpu.SemaphoreType.DMA
    in_vmem, anywhere = pl.BlockSpec(memory_space=pltpu.VMEM), pl.BlockSpec(memory_space=pl.ANY)
    gram, fibres = pl.pallas_call(
        functools.partial(gram_kernel, sizes),
        out_shape=(
            jax.ShapeDtypeStruct((variables, variables), jnp.float32),
            jax.ShapeDtypeStruct((variables, cells), jnp.bfloat16),
        ),
        in_specs=[anywhere],
        out_specs=(in_vmem, anywhere),
        scratch_shapes=[
            pltpu.VMEM((variables, cells), jnp.bfloat16),
            pltpu.VMEM((n_var, height, variables), jnp.float32),
            pltpu.VMEM((n_var, height, variables), jnp.float32),
            pltpu.VMEM((n_space, height, variables), jnp.float32),
            pltpu.VMEM((n_var, height, variables), jnp.float32),
            dma(()),
            dma((CHUNKS,)),
            dma((CHUNKS, n_var)),
            dma((CHUNKS, n_var)),
            dma((n_var,)),
            dma((n_var,)),
            dma((n_space,)),
            dma((n_space,)),
            dma((n_var,)),
            dma((n_var,)),
        ],
        compiler_params=pltpu.CompilerParams(
            collective_id=0, has_side_effects=True, vmem_limit_bytes=60 * 2**20
        ),
    )(tensor_field)
    basis, core = pl.pallas_call(
        core_kernel,
        out_shape=(
            jax.ShapeDtypeStruct((rank, variables), jnp.float32),
            jax.ShapeDtypeStruct((rank, cells), jnp.float32),
        ),
        in_specs=[in_vmem, in_vmem, anywhere],
        out_specs=(in_vmem, anywhere),
        scratch_shapes=[
            pltpu.VMEM((variables, cells), jnp.bfloat16),
            pltpu.VMEM((rank, cells), jnp.float32),
            pltpu.VMEM((len(RIGHT) * variables, variables), jnp.bfloat16),
            dma(()),
            dma((CHUNKS,)),
        ],
        compiler_params=pltpu.CompilerParams(vmem_limit_bytes=60 * 2**20),
    )(gram, start_basis.T, fibres)
    return basis.T, core


def solution(mesh):
    return jax.shard_map(
        functools.partial(per_device, dict(mesh.shape)),
        mesh=mesh,
        in_specs=(P("var", "space"), P()),
        out_specs=(P(), P(None, ("space", "var"))),
        check_vma=False,
    )
```
